32 devices in a mesh: grp: 16 (over z, x, core), narrow: 2 (over y).
Axes of the slice: x: 2, y: 2, z: 4, core: 2. Of those that a mesh axis runs over, the one named last changes fastest.
Arguments:
- block_input: bfloat16 [2, 2048, 1024], P('narrow', 'grp'), may hold values from -6 to 6
- proj_in: bfloat16 [1024, 4096], P(('grp', 'narrow')), may hold values from -0.1875 to 0.1875
- proj_gates: bfloat16 [1024, 16], P(('grp', 'narrow')), may hold values from -0.1875 to 0.1875
- proj_out: bfloat16 [1024, 1024], P(('grp', 'narrow')), may hold values from -0.375 to 0.375
- ffn_up: bfloat16 [1024, 5632], P(('grp', 'narrow')), may hold values from -0.1875 to 0.1875
- ffn_down: bfloat16 [2816, 1024], P(('grp', 'narrow')), may hold values from -0.109375 to 0.109375
- conv_taps: float32 [4, 3072], replicated, may hold values from -3 to 3
- attn_norm: float32 [1024], replicated, may hold values from 0.5 to 1.5
- out_norm: float32 [1024], replicated, may hold values from 0.5 to 1.5
- ffn_norm: float32 [1024], replicated, may hold values from 0.5 to 1.5
- decay_log: float32 [8], replicated, may hold values from -9.91 to -2.48
- doc_lengths: int32 [2, 3], P('narrow'), may hold values from 1 to 2046, as said below
- cotangent: bfloat16 [2, 2048, 1024], P('narrow', 'grp'), may hold values from -6 to 6
Outputs:
- block_output: bfloat16 [2, 2048, 1024], P('narrow', 'grp')
- input_grad: float32 [2, 2048, 1024], P('narrow', 'grp')
- grad_proj_in: float32 [1024, 4096], P(('grp', 'narrow'))
- grad_proj_gates: float32 [1024, 16], P(('grp', 'narrow'))
- grad_proj_out: float32 [1024, 1024], P(('grp', 'narrow'))
- grad_ffn_up: float32 [1024, 5632], P(('grp', 'narrow'))
- grad_ffn_down: float32 [2816, 1024], P(('grp', 'narrow'))
- grad_conv_taps: float32 [4, 3072], replicated
- grad_attn_norm: float32 [1024], replicated
- grad_out_norm: float32 [1024], replicated
- grad_ffn_norm: float32 [1024], replicated
- grad_decay_log: float32 [8], replicated
The draws below stay inside these ranges and needn't reach their ends.
Inputs may be any that keep to these rules, and one draw needn't show every extreme that they name: `doc_lengths`: each row lists the lengths of the 3 documents packed in order into one stream; they sum to 2048; the first document ends within the stream's first 128 tokens and the last one begins within its last 128 tokens.
All inputs are finite; a program needn't handle non-finite values.
Results may differ from the reference program's by a relative error of at most 0.012.
Values may be sent and summed in bfloat16 or wider, within the bound.
No kernel may reach another device: no remote copies, remote signals or barrier semaphores. Data moves between devices by JAX's collectives and lax.ppermute only.
A program may use at most 256 MiB of HBM per device.

```python
import jax
import jax.numpy as jnp
from jax import lax

D = 1024
HEADS = 8
HEAD_DIM = 128
FF = 2816
CONV = 4
CG_STEPS = 8
TOK_DEV = 128
STREAMS = 2
STREAM = 2048


def draw_decay_log(key, part):
    key = jax.random.fold_in(key, 5)
    fraction = jax.random.uniform(key, (HEADS,), jnp.float32)
    lowest = jnp.log(1.0 / 20000.0)
    highest = jnp.log(1.0 / 12.0)
    return (lowest + (highest - lowest) * fraction).astype(jnp.float32)


def draw_doc_lengths(key, part):
    opening = jax.random.randint(jax.random.fold_in(key, 11), (STREAMS, 1), 1, TOK_DEV, dtype=jnp.int32)
    closing = jax.random.randint(jax.random.fold_in(key, 23), (STREAMS, 1), 1, TOK_DEV, dtype=jnp.int32)
    chosen = jax.random.randint(jax.random.fold_in(key, 37), (), 0, STREAMS, dtype=jnp.int32)
    picked = (jnp.arange(STREAMS, dtype=jnp.int32) == chosen)[:, None]
    opening = jnp.where(picked, 1, opening).astype(jnp.int32)
    closing = jnp.where(picked, 1, closing).astype(jnp.int32)
    middle = STREAM - opening - closing
    return jnp.concatenate([opening, middle, closing], axis=1).astype(jnp.int32)


def steps_of(stream_key, shape, shards, low, high):
    loudness = 1.0
    for axis_at, shards_of in shards:
        steps = jax.random.uniform(jax.random.fold_in(jax.random.fold_in(stream_key, 6), axis_at), (shards_of,), jnp.float32, low / len(shards), high / len(shards))
        loudness = loudness * jnp.repeat(jnp.exp(steps), shape[axis_at] // shards_of).reshape((-1,) + (1,) * (len(shape) - 1 - axis_at))
    return loudness


def bell_draw(key, shape, scale, bound, shards=(), kind=jnp.bfloat16):
    values = jax.random.normal(key, shape, jnp.float32) * scale
    if len(shards) > 0:
        values = steps_of(key, shape, shards, -0.22, 0.18) * values
    return jnp.clip(values, min=-bound, max=bound).astype(kind)


def setup_inputs(seed: int = 0) -> dict:
    key_of = jax.random.split(jax.random.key(seed), 14)
    block_input = bell_draw(key_of[0], (STREAMS, STREAM, D), 1.0, 6.0, ((0, 2), (1, 16)))
    proj_in = bell_draw(key_of[1], (D, 4 * D), D ** -0.5, 0.1875, ((0, 32),))
    proj_gates = bell_draw(key_of[2], (D, 2 * HEADS), D ** -0.5, 0.1875, ((0, 32),))
    proj_out = bell_draw(key_of[3], (D, D), (D // 4) ** -0.5, 0.375, ((0, 32),))
    ffn_up = bell_draw(key_of[4], (D, 2 * FF), D ** -0.5, 0.1875, ((0, 32),))
    ffn_down = bell_draw(key_of[5], (FF, D), FF ** -0.5, 0.109375, ((0, 32),))
    conv_taps = bell_draw(key_of[6], (CONV, 3 * D), CONV ** -0.5, 3.0, (), jnp.float32)
    attn_norm = jnp.clip(1.0 + 0.1 * jax.random.normal(key_of[7], (D,), jnp.float32), 0.5, 1.5)
    out_norm = jnp.clip(1.0 + 0.1 * jax.random.normal(key_of[8], (D,), jnp.float32), 0.5, 1.5)
    ffn_norm = jnp.clip(1.0 + 0.1 * jax.random.normal(key_of[9], (D,), jnp.float32), 0.5, 1.5)
    decay_log = draw_decay_log(jax.random.fold_in(key_of[13], 71), 0)
    doc_lengths = draw_doc_lengths(jax.random.fold_in(key_of[13], 71), 0)
    cotangent = bell_draw(key_of[12], (STREAMS, STREAM, D), 1.0, 6.0, ((0, 2), (1, 16)))
    return dict(block_input=block_input, proj_in=proj_in, proj_gates=proj_gates, proj_out=proj_out, ffn_up=ffn_up, ffn_down=ffn_down, conv_taps=conv_taps, attn_norm=attn_norm, out_norm=out_norm, ffn_norm=ffn_norm, decay_log=decay_log, doc_lengths=doc_lengths, cotangent=cotangent)


EPSILON = 1e-06
CG_EPSILON = 1e-06
REGULARIZER = 16.0
PRECISE = lax.Precision.HIGHEST

@jax.custom_vjp
def low(v):
    return lax.optimization_barrier(v.astype(jnp.bfloat16)).astype(jnp.float32)

@jax.custom_vjp
def low_back(v):
    return v

def low_keep(v):
    return (low(v), None)

def low_pass(kept, grad):
    return (grad,)

def back_keep(v):
    return (v, None)

def back_low(kept, grad):
    return (low(grad),)
low.defvjp(low_keep, low_pass)
low_back.defvjp(back_keep, back_low)

def product(left, right):
    return jnp.dot(left, right, precision=PRECISE)

def rms_norm(values, norm_gain):
    return values * lax.rsqrt(lax.optimization_barrier(jnp.mean(values * values, axis=-1, keepdims=True)) + EPSILON) * norm_gain

def split_heads(flat_rows):
    return flat_rows.reshape(flat_rows.shape[0], HEADS, HEAD_DIM).transpose(1, 0, 2)

def join_heads(stacked):
    return stacked.transpose(1, 0, 2).reshape(stacked.shape[1], HEADS * HEAD_DIM)

def unit_heads(flat_rows):
    shaped = flat_rows.reshape(flat_rows.shape[0], HEADS, HEAD_DIM)
    scaled = shaped * lax.rsqrt(lax.optimization_barrier(jnp.sum(shaped * shaped, axis=-1, keepdims=True)) + EPSILON)
    return scaled.reshape(flat_rows.shape)

def conv_features(extended, conv_taps, place_docs):
    length = extended.shape[0] - (CONV - 1)
    own_docs = place_docs[CONV - 1:]
    summed = jnp.zeros((length, extended.shape[1]), jnp.float32)
    for offset in range(CONV):
        first_row = CONV - 1 - offset
        window = extended[first_row:first_row + length]
        same_doc = (place_docs[first_row:first_row + length] == own_docs).astype(jnp.float32)
        summed = summed + conv_taps[offset] * window * same_doc[:, None]
    activated = jax.nn.silu(summed)
    model_width = HEADS * HEAD_DIM
    return (unit_heads(activated[:, :model_width]), unit_heads(activated[:, model_width:2 * model_width]), activated[:, 2 * model_width:])

def gate_values(gate_logits, decay_log):
    log_decay = -jnp.exp(decay_log)[None, :] * jax.nn.sigmoid(gate_logits[:, :HEADS])
    return (log_decay, jax.nn.sigmoid(gate_logits[:, HEADS:]))

def decay_tables(log_decay, segments, carry_flag):
    cumulative = jnp.cumsum(log_decay, axis=0).T
    length = segments.shape[0]
    position = jnp.arange(length, dtype=jnp.int32)
    visible = (segments[:, None] == segments[None, :]) & (position[None, :] <= position[:, None])
    spread = jnp.exp(jnp.minimum(cumulative[:, :, None] - cumulative[:, None, :], 0.0)) * visible.astype(jnp.float32)[None]
    carried = ((segments == segments[0]) & carry_flag).astype(jnp.float32)
    entry_decay = jnp.exp(cumulative) * carried[None, :]
    last_doc = (segments == segments[length - 1]).astype(jnp.float32)
    tail_decay = jnp.exp(cumulative[:, length - 1:] - cumulative) * last_doc[None, :]
    return (spread, entry_decay, tail_decay)

def scale_state(factor, state_in):
    return factor[None, :, None, None] * state_in

def apply_system(probe_rows, key_heads, weights, entry_decay, curvature):
    carried_part = jnp.einsum('hck,hkl->hcl', probe_rows, curvature, precision=PRECISE) * entry_decay[:, :, None]
    scores = jnp.einsum('hck,hjk->hcj', probe_rows, key_heads, precision=PRECISE) * weights
    return REGULARIZER * probe_rows + carried_part + jnp.einsum('hcj,hjk->hck', scores, key_heads, precision=PRECISE)

def block_out(queries, key_rows, value_rows, log_decay, in_gate, state_in, segments, carry_flag):
    spread, entry_decay, tail_decay = decay_tables(log_decay, segments, carry_flag)
    weights = spread * in_gate.T[:, None, :]
    query_heads = split_heads(queries)
    key_heads = split_heads(key_rows)
    value_heads = split_heads(value_rows)
    solution = jnp.zeros_like(query_heads)
    residual = query_heads
    direction = query_heads
    norm_now = lax.optimization_barrier(jnp.sum(residual * residual, axis=-1, keepdims=True))
    for iteration in range(CG_STEPS):
        applied = apply_system(direction, key_heads, weights, entry_decay, state_in[0])
        step_size = norm_now / (lax.optimization_barrier(jnp.sum(direction * applied, axis=-1, keepdims=True)) + CG_EPSILON)
        solution = solution + step_size * direction
        residual = residual - step_size * applied
        if iteration + 1 < CG_STEPS:
            norm_next = lax.optimization_barrier(jnp.sum(residual * residual, axis=-1, keepdims=True))
            direction = residual + norm_next / (norm_now + CG_EPSILON) * direction
            norm_now = norm_next
    carried_part = jnp.einsum('hck,hvk->hcv', solution, state_in[1], precision=PRECISE) * entry_decay[:, :, None]
    scores = jnp.einsum('hck,hjk->hcj', solution, key_heads, precision=PRECISE) * weights
    return join_heads(carried_part + jnp.einsum('hcj,hjv->hcv', scores, value_heads, precision=PRECISE))

def block_summary(key_rows, value_rows, log_decay, in_gate, segments, carry_flag):
    spread, entry_decay, tail_decay = decay_tables(log_decay, segments, carry_flag)
    deposit = tail_decay * in_gate.T
    key_heads = split_heads(key_rows)
    value_heads = split_heads(value_rows)
    curvature = jnp.einsum('hc,hck,hcl->hkl', deposit, key_heads, key_heads, precision=PRECISE)
    coupling = jnp.einsum('hc,hcv,hck->hvk', deposit, value_heads, key_heads, precision=PRECISE)
    return (entry_decay[:, -1], jnp.stack([curvature, coupling]))

def out_gate(mesa_out, pre_gate, out_norm):
    per_head = mesa_out.reshape(mesa_out.shape[0], HEADS, HEAD_DIM)
    normed = per_head * lax.rsqrt(lax.optimization_barrier(jnp.mean(per_head * per_head, axis=-1, keepdims=True)) + EPSILON)
    return normed.reshape(mesa_out.shape) * out_norm * jax.nn.silu(pre_gate)

def swiglu(gate_up):
    return jax.nn.silu(gate_up[:, :FF]) * gate_up[:, FF:]

def mesa_stream(queries, key_rows, value_rows, log_decay, in_gate, segments):
    block_count = queries.shape[0] // TOK_DEV

    def as_blocks(source):
        return source.reshape((block_count, TOK_DEV) + source.shape[1:])
    before = jnp.concatenate([jnp.full((1,), -1, jnp.int32), segments[:-1]])
    carry_flags = as_blocks(segments)[:, 0] == as_blocks(before)[:, 0]

    def advance(state_in, members):
        query_block, key_block, value_block, decay_block, gate_block, doc_block, flag_block = members
        outcome = block_out(query_block, key_block, value_block, decay_block, gate_block, state_in, segments=doc_block, carry_flag=flag_block)
        through, fresh_state = block_summary(key_block, value_block, decay_block, gate_block, segments=doc_block, carry_flag=flag_block)
        return (scale_state(through, state_in) + fresh_state, outcome)
    initial = jnp.zeros((2, HEADS, HEAD_DIM, HEAD_DIM), jnp.float32)
    unused_state, outcomes = lax.scan(jax.checkpoint(advance), initial, (as_blocks(queries), as_blocks(key_rows), as_blocks(value_rows), as_blocks(log_decay), as_blocks(in_gate), as_blocks(segments), carry_flags))
    return outcomes.reshape(queries.shape[0], HEADS * HEAD_DIM)

def stream_layer(hidden_in, proj_in, proj_gates, proj_out, ffn_up, ffn_down, conv_taps, attn_norm, out_norm, ffn_norm, decay_log, segments):
    normed = low(rms_norm(hidden_in, attn_norm))
    projected = low_back(product(normed, jnp.concatenate([proj_in, proj_gates], axis=1)))
    features = projected[:, :3 * D]
    pre_gate = projected[:, 3 * D:4 * D]
    gate_logits = projected[:, 4 * D:]
    extended = jnp.concatenate([jnp.zeros((CONV - 1, 3 * D), jnp.float32), features], axis=0)
    place_docs = jnp.concatenate([jnp.full((CONV - 1,), -1, jnp.int32), segments])
    queries, key_rows, value_rows = conv_features(extended, conv_taps, place_docs)
    log_decay, in_gate = gate_values(gate_logits, decay_log)
    mesa_out = mesa_stream(queries, key_rows, value_rows, log_decay, in_gate, segments)
    gated_out = low(out_gate(mesa_out, pre_gate, out_norm))
    hidden = hidden_in + low_back(product(gated_out, proj_out))
    normed_two = low(rms_norm(hidden, ffn_norm))
    act_low = low(swiglu(low_back(product(normed_two, ffn_up))))
    return hidden + low_back(product(act_low, ffn_down))

def reference(block_input, proj_in, proj_gates, proj_out, ffn_up, ffn_down, conv_taps, attn_norm, out_norm, ffn_norm, decay_log, doc_lengths, cotangent):
    params = tuple((member.astype(jnp.float32) for member in (proj_in, proj_gates, proj_out, ffn_up, ffn_down, conv_taps, attn_norm, out_norm, ffn_norm, decay_log)))
    positions = jnp.arange(STREAM, dtype=jnp.int32)

    def per_stream(totals, stream_item):
        stream_input, stream_cot, stream_lengths = stream_item
        doc_ends = jnp.cumsum(stream_lengths)
        segments = lax.optimization_barrier(jnp.sum((positions[:, None] >= doc_ends[None, :]).astype(jnp.int32), axis=1))

        def forward(hidden_in, *weights):
            return stream_layer(hidden_in, *weights, segments)
        result, pullback = jax.vjp(forward, stream_input.astype(jnp.float32), *params)
        gradients = pullback(stream_cot.astype(jnp.float32))
        totals = tuple((first + second for first, second in zip(totals, gradients[1:])))
        return (totals, (result.astype(jnp.bfloat16), gradients[0]))
    initial = tuple((jnp.zeros_like(member) for member in params))
    totals, (outputs, input_grads) = lax.scan(per_stream, initial, (block_input, cotangent, doc_lengths))
    return (outputs, input_grads, totals[0], totals[1], totals[2], totals[3], totals[4], totals[5], totals[6], totals[7], totals[8], totals[9])
```

```python
import functools

import jax
import jax.numpy as jnp
from jax import lax
from jax.sharding import Mesh, PartitionSpec as P

D = 1024
HEADS = 8
HEAD_DIM = 128
FF = 2816
CONV = 4
CG_STEPS = 8

EPSILON = 1e-06
CG_EPSILON = 1e-06
REGULARIZER = 16.0
PRECISE = lax.Precision.HIGHEST
EVERY = ("out", "inn", "narrow")
BF = jnp.bfloat16
F32 = jnp.float32


def xor_permute(value, axis, distance):
    count = lax.axis_size(axis)
    return lax.ppermute(value, axis, [(source, source ^ distance) for source in range(count)])


def passed_along(value, steps):
    count = lax.axis_size("out")
    leading, last = (max(0, -steps), min(count, count - steps))
    return lax.ppermute(value, "out", [(source, source + steps) for source in range(leading, last)])


def butterfly_sum(value):
    for axis in EVERY:
        distance = 1
        while distance < lax.axis_size(axis):
            value = value + xor_permute(value, axis, distance)
            distance *= 2
    return value


def gather_pieces(mine):
    pieces = {0: mine, 1: xor_permute(mine, "inn", 1)}
    for distance in (2, 4, 6):
        pieces[distance] = xor_permute(mine, "inn", distance)
    for distance in (2, 4, 6):
        pieces[distance + 1] = xor_permute(pieces[distance], "inn", 1)
    return [pieces[k] for k in range(8)]


def gather_rows(mine):
    pieces = jnp.stack(gather_pieces(mine))
    order = jnp.arange(8, dtype=jnp.int32) ^ lax.axis_index("inn")
    return pieces[order].reshape((8 * mine.shape[0],) + mine.shape[1:])


def scatter_sum(parts):
    low = parts.astype(BF)
    me = lax.axis_index("inn")

    def block(k):
        return lax.dynamic_index_in_dim(low, me ^ k, 0, keepdims=False)

    paired = {
        k: block(k).astype(F32) + xor_permute(block(k + 1), "inn", 1).astype(F32) for k in (0, 2, 4, 6)
    }
    total = paired[0]
    for k in (2, 4, 6):
        total = total + xor_permute(paired[k].astype(BF), "inn", k).astype(F32)
    return total


def exchange(blocks, axes):
    return lax.all_to_all(blocks, axes, split_axis=0, concat_axis=0, tiled=True)


def rms_norm(values, norm_gain):
    return (
        values * lax.rsqrt(jnp.mean(values * values, axis=-1, keepdims=True) + EPSILON) * norm_gain
    )


def unit_rows(rows):
    return rows * lax.rsqrt(jnp.sum(rows * rows, axis=-1, keepdims=True) + EPSILON)


def conv_features(extended, conv_taps, place_docs):
    length = extended.shape[0] - (CONV - 1)
    own_docs = place_docs[CONV - 1 :]
    summed = jnp.zeros((length, extended.shape[1]), F32)
    for offset in range(CONV):
        first_row = CONV - 1 - offset
        window = extended[first_row : first_row + length]
        same_doc = (place_docs[first_row : first_row + length] == own_docs).astype(F32)
        summed = summed + conv_taps[offset] * window * same_doc[:, None]
    activated = jax.nn.silu(summed)
    return (
        unit_rows(activated[:, :HEAD_DIM]),
        unit_rows(activated[:, HEAD_DIM : 2 * HEAD_DIM]),
        activated[:, 2 * HEAD_DIM :],
    )


def gate_values(gate_logits, decay_log):
    log_decay = -jnp.exp(decay_log) * jax.nn.sigmoid(gate_logits[:, 0])
    return (log_decay, jax.nn.sigmoid(gate_logits[:, 1]))


def decay_tables(log_decay, segments, carry_flags):
    cumulative = jnp.cumsum(log_decay, axis=1)
    length = segments.shape[1]
    position = jnp.arange(length, dtype=jnp.int32)
    visible = (segments[:, :, None] == segments[:, None, :]) & (
        position[None, :] <= position[:, None]
    )[None]
    spread = jnp.exp(jnp.minimum(cumulative[:, :, None] - cumulative[:, None, :], 0.0)) * visible.astype(
        F32
    )
    carried = ((segments == segments[:, :1]) & carry_flags[:, None]).astype(F32)
    entry_decay = jnp.exp(cumulative) * carried
    last_doc = (segments == segments[:, length - 1 :]).astype(F32)
    tail_decay = jnp.exp(cumulative[:, length - 1 :] - cumulative) * last_doc
    return (spread, entry_decay, tail_decay)


def ein(spec, *operands):
    return jnp.einsum(spec, *operands, precision=PRECISE)


def apply_system(probe_rows, keys, weights, entry_decay, curvature):
    carried_part = ein("hck,hkl->hcl", probe_rows, curvature) * entry_decay[:, :, None]
    scores = ein("hck,hjk->hcj", probe_rows, keys) * weights
    return REGULARIZER * probe_rows + carried_part + ein("hcj,hjk->hck", scores, keys)


def block_out(queries, keys, values, log_decay, in_gate, state_in, segments, carry_flags):
    spread, entry_decay, tail_decay = decay_tables(log_decay, segments, carry_flags)
    weights = spread * in_gate[:, None, :]
    solution = jnp.zeros_like(queries)
    residual = queries
    direction = queries
    norm_now = jnp.sum(residual * residual, axis=-1, keepdims=True)
    for iteration in range(CG_STEPS):
        applied = apply_system(direction, keys, weights, entry_decay, state_in[0])
        step_size = norm_now / (jnp.sum(direction * applied, axis=-1, keepdims=True) + CG_EPSILON)
        solution = solution + step_size * direction
        residual = residual - step_size * applied
        if iteration + 1 < CG_STEPS:
            norm_next = jnp.sum(residual * residual, axis=-1, keepdims=True)
            direction = residual + norm_next / (norm_now + CG_EPSILON) * direction
            norm_now = norm_next
    carried_part = ein("hck,hvk->hcv", solution, state_in[1]) * entry_decay[:, :, None]
    scores = ein("hck,hjk->hcj", solution, keys) * weights
    return carried_part + ein("hcj,hjv->hcv", scores, values)


def block_summary(keys, values, log_decay, in_gate, segments, carry_flags):
    spread, entry_decay, tail_decay = decay_tables(log_decay, segments, carry_flags)
    deposit = tail_decay * in_gate
    curvature = ein("hc,hck,hcl->hkl", deposit, keys, keys)
    coupling = ein("hc,hcv,hck->hvk", deposit, values, keys)
    return (entry_decay[:, -1], jnp.stack([curvature, coupling]))


def out_gate(mesa_out, pre_gate, out_norm):
    normed = mesa_out * lax.rsqrt(jnp.mean(mesa_out * mesa_out, axis=-1, keepdims=True) + EPSILON)
    return normed * out_norm * jax.nn.silu(pre_gate)


def swiglu(gate_up):
    half = gate_up.shape[1] // 2
    return jax.nn.silu(gate_up[:, :half]) * gate_up[:, half:]


def dot32(left, right):
    return jnp.dot(left, right, preferred_element_type=F32)


def per_device(
    block_input,
    proj_in,
    proj_gates,
    proj_out,
    ffn_up,
    ffn_down,
    conv_taps,
    attn_norm,
    out_norm,
    ffn_norm,
    decay_log,
    doc_lengths,
    cotangent,
):
    outer = lax.axis_size("out")
    narrow = lax.axis_size("narrow")
    devices = outer * 8 * narrow
    me = lax.axis_index("inn")
    token_count = block_input.shape[1]
    group_tokens = 8 * token_count
    in_rows = proj_in.shape[0]
    units = ffn_down.shape[0]
    own_units = outer * narrow * units

    doc_ends = jnp.cumsum(doc_lengths[0])
    places = (
        lax.axis_index("out") * group_tokens
        - (CONV - 1)
        + jnp.arange(group_tokens + CONV - 1, dtype=jnp.int32)
    )
    counted = jnp.sum((places[:, None] >= doc_ends[None, :]).astype(jnp.int32), axis=1)
    place_docs = jnp.where(places >= 0, counted, -1)
    segments = place_docs[CONV - 1 :].reshape(8, token_count)
    carry_flags = segments[:, 0] == place_docs[CONV - 2 : -1].reshape(8, token_count)[:, 0]

    def for_heads(blocks):
        spread_out = jnp.broadcast_to(
            blocks[None, :, None], (outer, 8, narrow) + blocks.shape[1:]
        )
        return spread_out.reshape((devices,) + blocks.shape[1:])

    in_blocks = proj_in.reshape(in_rows, 4, 8, HEAD_DIM).transpose(2, 0, 1, 3)
    in_blocks = in_blocks.reshape(8, in_rows, 4 * HEAD_DIM)
    gate_blocks = proj_gates.reshape(in_rows, 2, 8).transpose(2, 0, 1)
    gate_blocks = jnp.pad(gate_blocks, ((0, 0), (0, 0), (0, HEAD_DIM - 2)))
    in_mine = exchange(for_heads(jnp.concatenate([in_blocks, gate_blocks], axis=2)), EVERY)
    in_mine = in_mine.reshape(D, 5 * HEAD_DIM)

    hidden_in = block_input[0].astype(F32)
    normed, norm_one_pull = jax.vjp(rms_norm, hidden_in, attn_norm)
    normed_all = gather_rows(normed.astype(BF))

    up_blocks = ffn_up.reshape(in_rows, 2, outer, 8, narrow, units).transpose(3, 0, 1, 2, 4, 5)
    up_mine = exchange(for_heads(up_blocks.reshape(8, in_rows, 2 * own_units)), EVERY)
    up_mine = up_mine.reshape(D, 2 * own_units)
    down_mine = lax.all_gather(ffn_down, ("out", "narrow"), axis=0, tiled=True)
    out_full = lax.all_gather(proj_out, EVERY, axis=0, tiled=True)
    grad_output = cotangent[0]
    grad_output_all = gather_rows(grad_output)

    projected = dot32(normed_all, in_mine)
    features = projected[:, : 3 * HEAD_DIM]
    pre_gate = projected[:, 3 * HEAD_DIM : 4 * HEAD_DIM]
    gate_logits = projected[:, 4 * HEAD_DIM : 4 * HEAD_DIM + 2]
    before_rows = passed_along(features[group_tokens - (CONV - 1) :], 1)
    extended = jnp.concatenate([before_rows, features], axis=0)
    own_taps = lax.dynamic_index_in_dim(
        conv_taps.reshape(CONV, 3, 8, HEAD_DIM), me, 2, keepdims=False
    ).reshape(CONV, 3 * HEAD_DIM)
    own_out_norm = lax.dynamic_slice_in_dim(out_norm, me * HEAD_DIM, HEAD_DIM)
    (queries, key_rows, value_rows), conv_pull = jax.vjp(
        functools.partial(conv_features, place_docs=place_docs), extended, own_taps
    )
    own_decay = lax.dynamic_index_in_dim(decay_log, me, 0, keepdims=False)
    (log_decay, in_gate), gate_pull = jax.vjp(gate_values, gate_logits, own_decay)

    def chunked(rows):
        return rows.reshape((8, token_count) + rows.shape[1:])

    queries, key_rows, value_rows, log_decay, in_gate = (
        chunked(queries),
        chunked(key_rows),
        chunked(value_rows),
        chunked(log_decay),
        chunked(in_gate),
    )
    tables = dict(segments=segments, carry_flags=carry_flags)
    (through, fresh), summary_pull = jax.vjp(
        functools.partial(block_summary, **tables), key_rows, value_rows, log_decay, in_gate
    )
    states = [jnp.zeros_like(fresh[:, 0])]
    reach = [jnp.ones((), F32)]
    for chunk in range(8):
        states.append(through[chunk] * states[-1] + fresh[:, chunk])
        reach.append(through[chunk] * reach[-1])
    arriving = jnp.zeros_like(states[0])
    for relay in range(outer - 1):
        arriving = passed_along(reach[8] * arriving + states[8], 1)
    incoming = jnp.stack([states[c] + reach[c] * arriving for c in range(8)], axis=1)
    mesa_out, out_pull = jax.vjp(
        functools.partial(block_out, **tables),
        queries,
        key_rows,
        value_rows,
        log_decay,
        in_gate,
        incoming,
    )
    gated_head, gate_out_pull = jax.vjp(
        out_gate, mesa_out.reshape(group_tokens, HEAD_DIM), pre_gate, own_out_norm
    )
    gated_low = lax.all_to_all(
        gated_head.astype(BF), "inn", split_axis=0, concat_axis=1, tiled=True
    )
    hidden = hidden_in + dot32(gated_low, out_full)
    normed_two, norm_two_pull = jax.vjp(rms_norm, hidden, ffn_norm)
    normed_two_all = gather_rows(normed_two.astype(BF))
    gate_up = dot32(normed_two_all, up_mine)
    activated, swiglu_pull = jax.vjp(swiglu, gate_up)
    act_low = activated.astype(BF)
    grad_act = dot32(grad_output_all, down_mine.T)
    (grad_gate_up,) = swiglu_pull(grad_act)
    grad_gate_low = grad_gate_up.astype(BF)
    grad_normed_two = scatter_sum(
        dot32(grad_gate_low, up_mine.T).reshape(8, token_count, D)
    )
    block_output = hidden + scatter_sum(dot32(act_low, down_mine).reshape(8, token_count, D))
    grad_hidden_norm, grad_ffn_norm = norm_two_pull(grad_normed_two)
    grad_hidden = grad_output.astype(F32) + grad_hidden_norm
    grad_branch = grad_hidden.astype(BF)
    grad_gated = dot32(grad_branch, out_full.T)
    grad_gated_head = lax.all_to_all(
        grad_gated.astype(BF), "inn", split_axis=1, concat_axis=0, tiled=True
    ).astype(F32)

    def owners_sum(parts):
        columns = parts.shape[1]
        received = exchange(parts.astype(BF).reshape(devices, in_rows, columns), EVERY)
        received = received.reshape(outer, 8, narrow, in_rows, columns)
        return jnp.sum(received.astype(F32), axis=(0, 2))

    up_sum = owners_sum(dot32(normed_two_all.T, grad_gate_low))
    grad_up = (
        up_sum.reshape(8, in_rows, 2, outer, narrow, units)
        .transpose(1, 2, 3, 0, 4, 5)
        .reshape(in_rows, 2 * FF)
    )
    down_parts = dot32(act_low.T, grad_output_all).astype(BF).reshape(outer * narrow, units, D)
    grad_down = jnp.sum(exchange(down_parts, ("out", "narrow")).astype(F32), axis=0)
    out_parts = dot32(gated_low.T, grad_branch).astype(BF).reshape(devices, in_rows, D)
    grad_out = jnp.sum(exchange(out_parts, EVERY).astype(F32), axis=0)

    grad_mesa, grad_pre_gate, grad_out_norm = gate_out_pull(grad_gated_head)
    grad_queries, grad_keys_out, grad_values_out, grad_decay_out, grad_gate_out, grad_incoming = (
        out_pull(chunked(grad_mesa))
    )
    later = jnp.zeros_like(arriving)
    for relay in range(outer - 1):
        total = later
        for chunk in reversed(range(8)):
            total = grad_incoming[:, chunk] + through[chunk] * total
        later = passed_along(total, -1)
    after = [later]
    for chunk in reversed(range(1, 8)):
        after.append(grad_incoming[:, chunk] + through[chunk] * after[-1])
    after_grad = jnp.stack(after[::-1], axis=1)
    grad_through = jnp.sum(after_grad * incoming, axis=(0, 2, 3))
    grad_keys_sum, grad_values_sum, grad_decay_sum, grad_gate_sum = summary_pull(
        (grad_through, after_grad)
    )

    def flat(rows):
        return rows.reshape((group_tokens,) + rows.shape[2:])

    grad_logits, grad_decay_log = gate_pull(
        (flat(grad_decay_out + grad_decay_sum), flat(grad_gate_out + grad_gate_sum))
    )
    grad_extended, grad_taps = conv_pull(
        (flat(grad_queries), flat(grad_keys_out + grad_keys_sum), flat(grad_values_out + grad_values_sum))
    )
    returned = passed_along(grad_extended[: CONV - 1], -1)
    grad_features = grad_extended[CONV - 1 :] + jnp.pad(
        returned, ((group_tokens - (CONV - 1), 0), (0, 0))
    )
    grad_projected = jnp.concatenate(
        [
            grad_features,
            grad_pre_gate,
            jnp.pad(grad_logits, ((0, 0), (0, HEAD_DIM - 2))),
        ],
        axis=1,
    ).astype(BF)
    grad_normed = scatter_sum(dot32(grad_projected, in_mine.T).reshape(8, token_count, D))
    grad_input_norm, grad_attn_norm = norm_one_pull(grad_normed)
    input_grad = grad_hidden + grad_input_norm
    in_sum = owners_sum(dot32(normed_all.T, grad_projected))
    grad_in = (
        in_sum[:, :, : 4 * HEAD_DIM]
        .reshape(8, in_rows, 4, HEAD_DIM)
        .transpose(1, 2, 0, 3)
        .reshape(in_rows, 4 * D)
    )
    grad_gates = (
        in_sum[:, :, 4 * HEAD_DIM : 4 * HEAD_DIM + 2].transpose(1, 2, 0).reshape(in_rows, 16)
    )

    own_head = jnp.arange(8, dtype=jnp.int32) == me
    head_parts = jnp.concatenate(
        [grad_taps.reshape(-1), grad_out_norm, jnp.broadcast_to(grad_decay_log, (HEAD_DIM,))]
    )
    head_parts = jnp.where(own_head[:, None], head_parts[None, :], 0.0)
    small = jnp.concatenate([head_parts.reshape(-1, HEAD_DIM), grad_attn_norm.reshape(-1, HEAD_DIM), grad_ffn_norm.reshape(-1, HEAD_DIM)])
    small = butterfly_sum(small)
    heads_rows = small[: 8 * (3 * CONV + 2)].reshape(8, 3 * CONV + 2, HEAD_DIM)
    taps_total = heads_rows[:, : 3 * CONV].reshape(8, CONV, 3, HEAD_DIM).transpose(1, 2, 0, 3)
    return (
        block_output.astype(BF)[None],
        input_grad[None],
        grad_in,
        grad_gates,
        grad_out,
        grad_up,
        grad_down,
        taps_total.reshape(CONV, 3 * D),
        small[8 * (3 * CONV + 2) :][:8].reshape(D),
        heads_rows[:, 3 * CONV].reshape(D),
        small[8 * (3 * CONV + 2) :][8:].reshape(D),
        heads_rows[:, 3 * CONV + 1, 0],
    )


def solution(mesh):
    fine = Mesh(
        mesh.devices.reshape(-1, 8, mesh.shape["narrow"]), EVERY
    )
    tokens = P("narrow", ("out", "inn"), None)
    rows = P(EVERY, None)
    return jax.shard_map(
        per_device,
        mesh=fine,
        in_specs=(tokens, rows, rows, rows, rows, rows)
        + (P(), P(), P(), P(), P())
        + (P("narrow", None), tokens),
        out_specs=(tokens, tokens, rows, rows, rows, rows, rows, P(), P(), P(), P(), P()),
        check_vma=False,
    )
```
